1024 devices in a mesh: ctx: 64 (over y_hi, z), exp: 8 (over x, core), rep: 2 (over y_lo).
Axes of the slice: x: 4, y: 8 (y_hi: 4, y_lo: 2; y = y_hi * 2 + y_lo), z: 16, core: 2. Of those that a mesh axis runs over, the one named last changes fastest.
Arguments:
- queries: bfloat16 [4096, 64, 576], P(('rep', 'exp'), 'ctx'), parts along dimension 0, may hold values from -2048 to 2048
- latents: bfloat16 [4096, 576], P(('rep', 'exp')), parts along dimension 0, may hold values from -6 to 6
- out_grad: bfloat16 [4096, 64, 512], P(('rep', 'exp'), 'ctx'), parts along dimension 0, may hold values from -24 to 24
Outputs:
- attended: bfloat16 [4096, 64, 512], P(('rep', 'exp'), 'ctx'), parts along dimension 0
- query_grad: float32 [4096, 64, 576], P(('rep', 'exp'), 'ctx'), parts along dimension 0
- latent_grad: float32 [4096, 576], P(('rep', 'exp')), parts along dimension 0
The draws below stay inside these ranges and needn't reach their ends.
There are 2 independent parts, one for each index of `rep`. The reference program is written for one: setup_inputs(seed, part) draws one part's arguments, and reference() takes and returns one part's arrays. A program takes and returns all parts, laid end to end along the dimension named above; each array names one. Nothing has to cross between parts.
All inputs are finite; a program needn't handle non-finite values.
Results may differ from the reference program's by a relative error of at most 0.013.
Values may be sent and summed in bfloat16 or wider, within the bound.
A program may use at most 64 MiB of HBM per device.

```python
import jax
import jax.numpy as jnp
from jax import lax

LATENT = 512
ROPE = 64
HEADS = 64
SEQ = 2048


def latent_base(key):
    return jnp.clip(jax.random.normal(key, (SEQ, LATENT + ROPE), jnp.float32), -6.0, 6.0)


def draw_latents(key, part):
    shared = latent_base(key)
    return shared.astype(jnp.bfloat16)


def draw_queries(key, part):
    key = jax.random.fold_in(key, 7)
    pieces = jax.random.split(key, 1)
    feature_width = LATENT + ROPE
    drawn = 0.5 * jnp.clip(jax.random.normal(pieces[0], (SEQ, HEADS, feature_width), jnp.float32), -6.0, 6.0)
    return drawn.astype(jnp.bfloat16)


def steps_of(rng, dims, shards, least, top_value):
    level = 1.0
    for axis_at, parts in shards:
        steps = jax.random.uniform(jax.random.fold_in(jax.random.fold_in(rng, 6), axis_at), (parts,), jnp.float32, least / len(shards), top_value / len(shards))
        level = level * jnp.repeat(jnp.exp(steps), dims[axis_at] // parts).reshape((-1,) + (1,) * (len(dims) - 1 - axis_at))
    return level


def gaussian(own_key, dims, deviation, limit, cuts=(), kind=jnp.bfloat16):
    entries = deviation * jax.random.normal(own_key, dims, jnp.float32)
    if cuts:
        entries = entries * steps_of(own_key, dims, cuts, -0.22, 0.18)
    return jnp.clip(entries, -limit, limit).astype(kind)


def setup_inputs(seed: int = 0, part: int = 0) -> dict:
    splits = jax.random.split(jax.random.key(seed), 4)
    own_keys = jax.random.split(jax.random.fold_in(splits[3], part), 4)
    return {
        "queries": draw_queries(jax.random.fold_in(jax.random.fold_in(splits[3], part), 71), part),
        "latents": draw_latents(jax.random.fold_in(jax.random.fold_in(splits[3], part), 71), part),
        "out_grad": gaussian(own_keys[2], (SEQ, HEADS, LATENT), 4.0, 24.0, ((0, 8), (1, 64))),
    }


score_scale = 192.0 ** -0.5


def reference(queries, latents, out_grad):
    values = latents[:, :LATENT]
    positions = jnp.arange(SEQ, dtype=jnp.int32)
    allowed = positions[None, :] <= positions[:, None]

    def one_head(summed, inputs):
        query_head, grad_head = inputs
        scores = jnp.dot(query_head, latents.T, preferred_element_type=jnp.float32) * score_scale
        scores = jnp.where(allowed, scores, -1e30)
        row_top = jnp.max(scores, axis=1, keepdims=True)
        row_mass = jnp.sum(jnp.exp(scores - row_top), axis=1, keepdims=True)
        probs = jnp.where(allowed, jnp.exp(scores - (row_top + jnp.log(row_mass))), 0.0)
        weights = probs.astype(jnp.bfloat16)
        context = jnp.dot(weights, values, preferred_element_type=jnp.float32)
        prob_grad = jnp.dot(grad_head, values.T, preferred_element_type=jnp.float32)
        row_delta = jnp.sum(grad_head.astype(jnp.float32) * context, axis=1, keepdims=True)
        score_grad = (probs * (prob_grad - row_delta)).astype(jnp.bfloat16)
        query_grad = jnp.dot(score_grad, latents, preferred_element_type=jnp.float32) * score_scale
        key_part = jnp.dot(score_grad.T, query_head, preferred_element_type=jnp.float32) * score_scale
        value_part = jnp.dot(weights.T, grad_head, preferred_element_type=jnp.float32)
        key_part = key_part + jnp.pad(value_part, ((0, 0), (0, ROPE)))
        return summed + key_part, (context.astype(jnp.bfloat16), query_grad)

    start_grad = jnp.zeros((SEQ, LATENT + ROPE), jnp.float32)
    latent_grad, (attended, query_grad) = lax.scan(
        one_head, start_grad, (jnp.swapaxes(queries, 0, 1), jnp.swapaxes(out_grad, 0, 1)))
    return jnp.swapaxes(attended, 0, 1), jnp.swapaxes(query_grad, 0, 1), latent_grad
```

```python
import functools

import jax
import jax.numpy as jnp
from jax import lax
from jax.experimental import pallas as pl
from jax.experimental.pallas import tpu as pltpu
from jax.sharding import PartitionSpec as P

MESH = pl.DeviceIdType.MESH
BF = jnp.bfloat16
F32 = jnp.float32
score_scale = 192.0 ** (-0.5)
NN = (((1,), (0,)), ((), ()))
NT = (((1,), (1,)), ((), ()))


def mm(a, b, dims=NN):
    return lax.dot_general(a, b, dims, preferred_element_type=F32)


def kernel(
    qt_ref, lt_ref, g_ref,
    att_ref, qg_ref, lg_ref,
    keys, qn, gt, sc, pg, ctx, row_m, row_l,
    sib_out, sib_in, hold, x_out, x_in, total,
    s1_out, s1_in, part1, s2_out, s2_in, part2, s3, g2, g1,
    ag_s, ag_r, fs_s, fs_r, cr_s, cr_r, xr_s, xr_r,
    s1_s, s1_r, s2_s, s2_r, s3_s, s3_r, g2_s, g2_r, g1_s, g1_r,
):
    c = lax.axis_index("ctx")
    e = lax.axis_index("exp")
    yh, z = c // 16, c % 16
    zi, zo = z % 4, z // 4
    x, k = e // 2, e % 2
    feat, rows = lt_ref.shape
    lat = g_ref.shape[1]

    sib = {"exp": x * 2 + (1 - k)}

    def at_x(v):
        return {"exp": v * 2 + k}

    def at_y(v):
        return {"ctx": v * 16 + z}

    def at_zi(v):
        return {"ctx": yh * 16 + zo * 4 + v}

    def at_zo(v):
        return {"ctx": yh * 16 + v * 4 + zi}

    a_me = jnp.where(k == 0, yh, zi)
    b_me = jnp.where(k == 0, zi, yh)

    def at_a(v):
        return {"ctx": jnp.where(k == 0, v * 16 + z, yh * 16 + zo * 4 + v)}

    def at_b(v):
        return {"ctx": jnp.where(k == 0, yh * 16 + zo * 4 + v, v * 16 + z)}

    def rdma(src, dst, ssem, rsem, dev):
        return pltpu.make_async_remote_copy(
            src_ref=src, dst_ref=dst, send_sem=ssem, recv_sem=rsem, device_id=dev, device_id_type=MESH
        )

    barrier = pltpu.get_barrier_semaphore()
    pl.semaphore_signal(barrier, inc=1, device_id=sib, device_id_type=MESH)
    for d in (1, 2, 3):
        pl.semaphore_signal(barrier, inc=1, device_id=at_x((x + d) % 4), device_id_type=MESH)
        pl.semaphore_signal(barrier, inc=1, device_id=at_y((yh + d) % 4), device_id_type=MESH)
        pl.semaphore_signal(barrier, inc=1, device_id=at_zi((zi + d) % 4), device_id_type=MESH)
        pl.semaphore_signal(barrier, inc=1, device_id=at_zo((zo + d) % 4), device_id_type=MESH)
    pl.semaphore_wait(barrier, 13)

    def ag(src_x, dst_x):
        return rdma(lt_ref, keys.at[src_x * 2 + k], ag_s.at[dst_x], ag_r.at[src_x], at_x(dst_x))

    for v in (1, 2, 3):
        @pl.when(v > x)
        def _():
            ag(x, v).start()

    own_fwd = rdma(lt_ref, keys.at[x * 2], fs_s.at[x], fs_r.at[x], sib)

    @pl.when(k == 0)
    def _():
        own_fwd.start()

    keys[e] = lt_ref[...]
    qn[...] = qt_ref[...].T
    gt[...] = g_ref[...].T

    below = lax.broadcasted_iota(jnp.int32, (rows, rows), 1) <= lax.broadcasted_iota(jnp.int32, (rows, rows), 0)
    s = jnp.where(below, mm(qn[...], lt_ref[...]) * score_scale, -1e30)
    sc[e] = s
    m = jnp.max(s, axis=1, keepdims=True)
    p = jnp.exp(s - m)
    row_m[...] = m
    row_l[...] = jnp.sum(p, axis=1, keepdims=True)
    ctx[...] = mm(p.astype(BF), lt_ref[:lat, :], NT)
    pg[e] = mm(g_ref[...], lt_ref[:lat, :])

    def forward(j):
        s = mm(qn[...], keys[j]) * score_scale
        sc[j] = s
        m_old = row_m[...]
        m = jnp.maximum(m_old, jnp.max(s, axis=1, keepdims=True))
        p = jnp.exp(s - m)
        fade = jnp.exp(m_old - m)
        row_m[...] = m
        row_l[...] = row_l[...] * fade + jnp.sum(p, axis=1, keepdims=True)
        ctx[...] = ctx[...] * fade + mm(p.astype(BF), keys[j, :lat, :], NT)
        pg[j] = mm(g_ref[...], keys[j, :lat, :])

    @pl.when(k == 1)
    def _():
        own_fwd.wait_recv()
        forward(x * 2)

    def pass_on(v, side):
        blk = keys.at[v * 2 + side]
        return rdma(blk, blk, fs_s.at[v], fs_r.at[v], sib)

    def fwd_step(v, carry):
        rdma(lt_ref, keys.at[v * 2 + k], ag_s.at[v], ag_r.at[v], at_x(v)).wait_recv()
        pass_on(v, k).start()
        forward(v * 2 + k)
        pass_on(v, 1 - k).wait_recv()
        forward(v * 2 + 1 - k)
        return carry

    lax.fori_loop(0, x, fwd_step, 0)

    inv = 1.0 / row_l[...]
    context = ctx[...] * inv
    att_ref[...] = context.astype(BF)
    lse = row_m[...] + jnp.log(row_l[...])
    delta = jnp.sum(g_ref[...].astype(F32) * context, axis=1, keepdims=True)
    row_m[...] = lse
    row_l[...] = delta
    qg_ref[...] = jnp.zeros_like(qg_ref)

    def backward(j, store):
        p = jnp.exp(sc[j] - row_m[...])
        ds = (p * (pg[j] - row_l[...])).astype(BF)
        qg_ref[...] += mm(keys[j], ds, NT)
        store(0, lat, mm(qt_ref[:lat, :], ds) * score_scale + mm(gt[...], p.astype(BF)))
        store(lat, feat, mm(qt_ref[lat:, :], ds) * score_scale)

    def to_sib(v):
        return rdma(sib_out.at[v], sib_in.at[v], cr_s.at[v], cr_r.at[v], sib)

    def to_x(v, src):
        return rdma(x_out.at[v], x_in.at[src], xr_s.at[v], xr_r.at[src], at_x(v))

    def bwd_pair(v):
        def put_sib(lo, hi, val):
            sib_out[v, lo:hi, :] = val.astype(BF)

        def put_hold(lo, hi, val):
            hold[v, lo:hi, :] = val

        backward(v * 2 + 1 - k, put_sib)
        to_sib(v).start()
        backward(v * 2 + k, put_hold)

    def send_x(v):
        to_sib(v).wait_recv()
        x_out[v] = (hold[v] + sib_in[v].astype(F32)).astype(BF)
        to_x(v, x).start()

    def bwd_step(v, carry):
        bwd_pair(v)

        @pl.when(v > 0)
        def _():
            send_x(v - 1)

        return carry

    lax.fori_loop(0, x, bwd_step, 0)

    @pl.when(k == 1)
    def _():
        def put_sib(lo, hi, val):
            sib_out[x, lo:hi, :] = val.astype(BF)

        backward(x * 2, put_sib)
        to_sib(x).start()

    @pl.when(x > 0)
    def _():
        send_x(x - 1)

    def put_total(lo, hi, val):
        total[lo:hi, :] = val

    backward(e, put_total)
    total[feat:, :] = jnp.zeros((total.shape[0] - feat, rows), F32)
    qg_ref[...] = qg_ref[...] * score_scale

    @pl.when(k == 0)
    def _():
        to_sib(x).wait_recv()
        total[:feat, :] += sib_in[x].astype(F32)

    def add_x(i, carry):
        v = 3 - i
        to_x(x, v).wait_recv()
        total[:feat, :] += x_in[v].astype(F32)
        return carry

    lax.fori_loop(0, 3 - x, add_x, 0)

    n1 = total.shape[0] // 4

    def c1(peer, src):
        return rdma(s1_out.at[peer], s1_in.at[src], s1_s.at[peer], s1_r.at[src], at_a(peer))

    for q in range(4):
        s1_out[q] = total[q * n1:(q + 1) * n1, :].astype(BF)
    for d in (1, 2, 3):
        c1((a_me + d) % 4, a_me).start()
    part1[...] = total[pl.ds(pl.multiple_of(a_me * n1, n1), n1), :]
    for d in (3, 2, 1):
        v = (a_me + d) % 4
        c1(a_me, v).wait_recv()
        part1[...] += s1_in[v].astype(F32)

    n2 = n1 // 2
    half = rows // 2

    def c2(peer, src):
        return rdma(s2_out.at[peer], s2_in.at[src], s2_s.at[peer], s2_r.at[src], at_b(peer))

    for q in range(4):
        lo, le = (q // 2) * n2, (q % 2) * half
        val = part1[lo:lo + n2, le:le + half]
        s2_out[q] = val.astype(BF)

        @pl.when(b_me == q)
        def _():
            part2[...] = val

    for d in (1, 2, 3):
        c2((b_me + d) % 4, b_me).start()
    for d in (3, 2, 1):
        v = (b_me + d) % 4
        c2(b_me, v).wait_recv()
        part2[...] += s2_in[v].astype(F32)

    def c3(peer, src):
        return rdma(s3.at[src], s3.at[src], s3_s.at[peer], s3_r.at[src], at_zo(peer))

    s3[zo] = part2[...].astype(BF)
    for d in (2, 1, 3):
        c3((zo + d) % 4, zo).start()
    for d in (1, 3, 2):
        c3(zo, (zo + d) % 4).wait_recv()
    g2[b_me] = (s3[0].astype(F32) + s3[1].astype(F32) + s3[2].astype(F32) + s3[3].astype(F32)).astype(BF)

    def c4(peer, src):
        return rdma(g2.at[src], g2.at[src], g2_s.at[peer], g2_r.at[src], at_b(peer))

    for d in (1, 2, 3):
        c4((b_me + d) % 4, b_me).start()
    for d in (3, 2, 1):
        c4(b_me, (b_me + d) % 4).wait_recv()
    for q in range(4):
        lo, le = (q // 2) * n2, (q % 2) * half
        g1[a_me, lo:lo + n2, le:le + half] = g2[q]

    def c5(peer, src):
        return rdma(g1.at[src], g1.at[src], g1_s.at[peer], g1_r.at[src], at_a(peer))

    for d in (1, 2, 3):
        c5((a_me + d) % 4, a_me).start()
    for d in (3, 2, 1):
        c5(a_me, (a_me + d) % 4).wait_recv()
    for q in range(4):
        hi = min(feat, (q + 1) * n1)
        lg_ref[q * n1:hi, :] = g1[q, :hi - q * n1, :].astype(F32)

    for v in (1, 2, 3):
        @pl.when(v > x)
        def _():
            ag(x, v).wait_send()

    @pl.when(k == 0)
    def _():
        own_fwd.wait_send()

    @pl.when(k == 1)
    def _():
        to_sib(x).wait_send()

    def drain(v, carry):
        pass_on(v, k).wait_send()
        to_sib(v).wait_send()
        to_x(v, x).wait_send()
        return carry

    lax.fori_loop(0, x, drain, 0)
    for d in (1, 2, 3):
        c1((a_me + d) % 4, a_me).wait_send()
        c2((b_me + d) % 4, b_me).wait_send()
        c3((zo + d) % 4, zo).wait_send()
        c4((b_me + d) % 4, b_me).wait_send()
        c5((a_me + d) % 4, a_me).wait_send()


def body(queries, latents, out_grad):
    rows, _, feat = queries.shape
    lat = out_grad.shape[2]
    padded = (feat + 127) // 128 * 128
    n1, n2 = padded // 4, padded // 8
    qt = queries.reshape(rows, feat).T
    vm = pltpu.VMEM
    sems = [pltpu.SemaphoreType.DMA((4,))] * 18
    att, qg, lg = pl.pallas_call(
        kernel,
        out_shape=(
            jax.ShapeDtypeStruct((rows, lat), BF),
            jax.ShapeDtypeStruct((feat, rows), F32),
            jax.ShapeDtypeStruct((feat, rows), F32),
        ),
        in_specs=[pl.BlockSpec(memory_space=pltpu.VMEM)] * 3,
        out_specs=[pl.BlockSpec(memory_space=pltpu.VMEM)] * 3,
        scratch_shapes=[
            vm((8, feat, rows), BF),
            vm((rows, feat), BF),
            vm((lat, rows), BF),
            vm((8, rows, rows), F32),
            vm((8, rows, rows), F32),
            vm((rows, lat), F32),
            vm((rows, 1), F32),
            vm((rows, 1), F32),
            vm((4, feat, rows), BF),
            vm((4, feat, rows), BF),
            vm((4, feat, rows), F32),
            vm((4, feat, rows), BF),
            vm((4, feat, rows), BF),
            vm((padded, rows), F32),
            vm((4, n1, rows), BF),
            vm((4, n1, rows), BF),
            vm((n1, rows), F32),
            vm((4, n2, rows // 2), BF),
            vm((4, n2, rows // 2), BF),
            vm((n2, rows // 2), F32),
            vm((4, n2, rows // 2), BF),
            vm((4, n2, rows // 2), BF),
            vm((4, n1, rows), BF),
        ] + sems,
        compiler_params=pltpu.CompilerParams(
            collective_id=0, has_side_effects=True, vmem_limit_bytes=48 * 2**20
        ),
    )(qt, latents.T, out_grad.reshape(rows, lat))
    return att.reshape(rows, 1, lat), qg.T.reshape(rows, 1, feat), lg.T


def solution(mesh):
    return jax.shard_map(
        body,
        mesh=mesh,
        in_specs=(
            P(("rep", "exp"), "ctx", None),
            P(("rep", "exp"), None),
            P(("rep", "exp"), "ctx", None),
        ),
        out_specs=(
            P(("rep", "exp"), "ctx", None),
            P(("rep", "exp"), "ctx", None),
            P(("rep", "exp"), None),
        ),
        check_vma=False,
    )
```

```python
import functools

import jax
import jax.numpy as jnp
from jax import lax
from jax.experimental import pallas as pl
from jax.experimental.pallas import tpu as pltpu
from jax.sharding import PartitionSpec as P

MESH = pl.DeviceIdType.MESH
BF = jnp.bfloat16
F32 = jnp.float32
score_scale = 192.0 ** (-0.5)
NN = (((1,), (0,)), ((), ()))
NT = (((1,), (1,)), ((), ()))
(AG, AH, ZU, ZD, FS, CR, RU, RD, XR, S1, S3, G1, G0) = range(0, 26, 2)


def mm(a, b, dims=NN):
    return lax.dot_general(a, b, dims, preferred_element_type=F32)


def at(start, size):
    return pl.ds(pl.multiple_of(start, 16), size)


def kernel(
    qt_any, lt_any, g_any,
    att_any, qg_any, lg_any,
    att_ref, qg_ref, fin,
    qt_ref, lt_ref, g_ref,
    keys, qn, gt, sc, pg, ctx, row_m, row_l,
    sib_out, sib_in, hold, z_out, z_in, x_out, x_in, total,
    s1_out, s1_in, part, s3, g1,
    in_sem, out_sem, sem, far,
):
    c = lax.axis_index("ctx")
    e = lax.axis_index("exp")
    yh, z = c // 16, c % 16
    zi, zo = z % 4, z // 4
    h, r = z % 2, zi // 2
    x, k = e // 2, e % 2
    feat, rows = lt_ref.shape
    lat = g_ref.shape[1]
    n_half, n_quarter = feat // 2, feat // 4
    mine, other = h * n_half, (1 - h) * n_half

    loads = [
        pltpu.make_async_copy(src, dst, in_sem.at[i])
        for i, (src, dst) in enumerate(((lt_any, lt_ref), (qt_any, qt_ref), (g_any, g_ref)))
    ]
    for load in loads:
        load.start()
    stores = [
        pltpu.make_async_copy(src, dst, out_sem.at[i])
        for i, (src, dst) in enumerate(((att_ref, att_any), (qg_ref, qg_any), (fin, lg_any)))
    ]

    sib = {"exp": x * 2 + (1 - k)}
    up, down = {"ctx": yh * 16 + (z + 1) % 16}, {"ctx": yh * 16 + (z + 15) % 16}
    def at_x(v):
        return {"exp": v * 2 + k}

    def at_shard(v):
        return {"ctx": (v // 2) * 16 + zo * 4 + (v % 2) * 2 + h}

    own = yh * 2 + r

    def at_zo(v):
        return {"ctx": yh * 16 + v * 4 + zi}

    def rdma(src, dst, kind, i, j, dev):
        return pltpu.make_async_remote_copy(
            src_ref=src, dst_ref=dst, send_sem=sem.at[kind, i], recv_sem=sem.at[kind + 1, j],
            device_id=dev, device_id_type=MESH,
        )

    barrier = pltpu.get_barrier_semaphore()
    near = [sib, up, down, at_zo((zo + 1) % 4), at_zo((zo + 3) % 4)]
    near += [at_x((x + d) % 4) for d in (1, 2, 3)] + [at_shard((own + d) % 8) for d in range(1, 8)]
    for dev in near:
        pl.semaphore_signal(barrier, inc=1, device_id=dev, device_id_type=MESH)
    loads[0].wait()
    keys[e] = lt_ref[...]
    pl.semaphore_wait(barrier, len(near))
    pl.semaphore_signal(far, inc=1, device_id=at_zo((zo + 1) % 4), device_id_type=MESH)

    def ag(src_x, dst_x, piece):
        part = at(mine + piece * n_quarter, n_quarter)
        return rdma(
            lt_ref.at[part], keys.at[src_x * 2 + k, part], AG if piece == 0 else AH, dst_x, src_x, at_x(dst_x)
        )

    def pass_on(v, side):
        blk = keys.at[v * 2 + side]
        return rdma(blk, blk, FS, v, v, sib)

    def lift(v, base):
        blk = keys.at[v * 2 + k, at(base, n_quarter)]
        return rdma(blk, blk, ZU, v, v, up)

    def lower(v, base):
        blk = keys.at[v * 2 + k, at(base + n_quarter, n_quarter)]
        return rdma(blk, blk, ZD, v, v, down)

    own_fwd = rdma(lt_ref, keys.at[x * 2], FS, x, x, sib)

    for piece in (0, 1):
        @pl.when(x < 3)
        def _():
            ag(x, x + 1, piece).start()

        @pl.when(x == 0)
        def _():
            ag(x, x + 3, piece).start()

    @pl.when(k == 0)
    def _():
        own_fwd.start()

    loads[1].wait()
    qn[...] = qt_ref[...].T
    loads[2].wait()
    gt[...] = g_ref[...].T

    below = lax.broadcasted_iota(jnp.int32, (rows, rows), 1) <= lax.broadcasted_iota(jnp.int32, (rows, rows), 0)
    s = jnp.where(below, mm(qn[...], lt_ref[...]) * score_scale, -1e30)
    sc[e] = s
    m = jnp.max(s, axis=1, keepdims=True)
    p = jnp.exp(s - m)
    row_m[...] = m
    row_l[...] = jnp.sum(p, axis=1, keepdims=True)
    ctx[...] = mm(p.astype(BF), lt_ref[:lat, :], NT)
    pg[e] = mm(g_ref[...], lt_ref[:lat, :])

    @pl.when(x < 2)
    def _():
        for piece in (0, 1):
            ag(x, x + 1, piece).wait_send()

            @pl.when(x == 0)
            def _():
                ag(x, x + 3, piece).wait_send()

            ag(x, x + 2, piece).start()

    def forward(j):
        s = mm(qn[...], keys[j]) * score_scale
        sc[j] = s
        m_old = row_m[...]
        m = jnp.maximum(m_old, jnp.max(s, axis=1, keepdims=True))
        p = jnp.exp(s - m)
        fade = jnp.exp(m_old - m)
        row_m[...] = m
        row_l[...] = row_l[...] * fade + jnp.sum(p, axis=1, keepdims=True)
        ctx[...] = ctx[...] * fade + mm(p.astype(BF), keys[j, :lat, :], NT)
        pg[j] = mm(g_ref[...], keys[j, :lat, :])

    @pl.when(k == 1)
    def _():
        own_fwd.wait_recv()
        forward(x * 2)

    def gather_step(i, carry):
        v = x - jnp.where(i == 0, 1, jnp.where(i == 1, 3, 2))

        @pl.when((i < 3) & (v >= 0))
        def _():
            ag(v, x, 0).wait_recv()
            lift(v, mine).start()
            ag(v, x, 1).wait_recv()
            lower(v, mine).start()

        w = x - jnp.where(i == 1, 1, jnp.where(i == 2, 3, 2))

        @pl.when((i > 0) & (w >= 0))
        def _():
            lift(w, other).wait_recv()
            lower(w, other).wait_recv()
            pass_on(w, k).start()
            forward(w * 2 + k)
            pass_on(w, 1 - k).wait_recv()
            forward(w * 2 + 1 - k)

        return carry

    lax.fori_loop(0, 4, gather_step, 0)

    inv = 1.0 / row_l[...]
    context = ctx[...] * inv
    att_ref[...] = context.astype(BF)
    stores[0].start()
    lse = row_m[...] + jnp.log(row_l[...])
    delta = jnp.sum(g_ref[...].astype(F32) * context, axis=1, keepdims=True)
    row_m[...] = lse
    row_l[...] = delta
    qg_ref[...] = jnp.zeros_like(qg_ref)

    def backward(j, store):
        p = jnp.exp(sc[j] - row_m[...])
        ds = (p * (pg[j] - row_l[...])).astype(BF)
        qg_ref[...] += mm(keys[j], ds, NT)
        store(0, lat, mm(qt_ref[:lat, :], ds) * score_scale + mm(gt[...], p.astype(BF)))
        store(lat, feat, mm(qt_ref[lat:, :], ds) * score_scale)

    def to_sib(v):
        return rdma(sib_out.at[v], sib_in.at[v], CR, v, v, sib)

    def to_up(v):
        return rdma(z_out.at[v, pl.ds(n_quarter, n_quarter)], z_in.at[v, pl.ds(n_quarter, n_quarter)], RU, v, v, up)

    def to_down(v):
        return rdma(z_out.at[v, pl.ds(0, n_quarter)], z_in.at[v, pl.ds(0, n_quarter)], RD, v, v, down)

    def to_x(v, src):
        return rdma(x_out.at[v], x_in.at[src], XR, v, src, at_x(v))

    def order(i):
        return x - jnp.where(i == 0, 2, jnp.where(i == 1, 3, jnp.where(i == 2, 1, 0)))

    def bwd_step(i, carry):
        v = order(i)

        @pl.when((i < 4) & (v >= 0))
        def _():
            def put_sib(lo, hi, val):
                sib_out[v, lo:hi, :] = val.astype(BF)

            def put_hold(lo, hi, val):
                hold[v, lo:hi, :] = val

            @pl.when(v * 2 + 1 - k <= e)
            def _():
                backward(v * 2 + 1 - k, put_sib)
                to_sib(v).start()

            backward(v * 2 + k, put_hold)

        u = order(i - 1)

        @pl.when((i > 0) & (i < 5) & (u >= 0))
        def _():
            @pl.when(u * 2 + k <= x * 2 + 1 - k)
            def _():
                to_sib(u).wait_recv()
                hold[u] += sib_in[u].astype(F32)

            z_out[u] = hold[u, at(other, n_half), :].astype(BF)
            to_up(u).start()
            to_down(u).start()

        t = order(i - 2)

        @pl.when((i > 1) & (t >= 0))
        def _():
            to_down(t).wait_recv()
            to_up(t).wait_recv()
            val = hold[t, at(mine, n_half), :] + z_in[t].astype(F32)

            @pl.when(t < x)
            def _():
                x_out[t] = val.astype(BF)
                to_x(t, x).start()

            @pl.when(t == x)
            def _():
                total[...] = val

        return carry

    lax.fori_loop(0, 6, bwd_step, 0)
    qg_ref[...] = qg_ref[...] * score_scale
    stores[1].start()

    def add_x(i, carry):
        v = 3 - i
        to_x(x, v).wait_recv()
        total[...] += x_in[v].astype(F32)
        return carry

    lax.fori_loop(0, 3 - x, add_x, 0)

    half = rows // 2
    n1, n2 = n_half // 2, s1_out.shape[1]

    def c1(peer, src):
        return rdma(s1_out.at[peer], s1_in.at[src], S1, peer, src, at_shard(peer))

    for q in range(8):
        lo = (q // 4) * n1 + (q % 2) * (n1 - n2)
        val = total[lo:lo + n2, (q // 2 % 2) * half:(q // 2 % 2 + 1) * half]
        s1_out[q] = val.astype(BF)

        @pl.when(own == q)
        def _():
            part[...] = val

    hops = (4, 5, 3, 2, 6, 7, 1)
    for d in hops:
        c1((own + d) % 8, own).start()
    for d in hops[::-1]:
        v = (own + d) % 8
        c1(own, v).wait_recv()
        part[...] += s1_in[v].astype(F32)

    def c3(peer, src):
        return rdma(s3.at[src], s3.at[src], S3, peer, src, at_zo(peer))

    s3[zo] = part[...].astype(BF)
    pl.semaphore_wait(far, 1)
    for d in (2, 1, 3):
        c3((zo + d) % 4, zo).start()
    for d in (1, 3, 2):
        c3(zo, (zo + d) % 4).wait_recv()
    g1[own] = (s3[0].astype(F32) + s3[1].astype(F32) + s3[2].astype(F32) + s3[3].astype(F32)).astype(BF)

    def c5(peer, src):
        return rdma(g1.at[src], g1.at[src], G1, peer, src, at_shard(peer))

    for d in hops:
        c5((own + d) % 8, own).start()
    for d in hops[::-1]:
        c5(own, (own + d) % 8).wait_recv()
    for q in range(8):
        skip = 0 if q % 2 == 0 else 2 * n2 - n1
        lo = (q // 4) * n1 + (q % 2) * n2
        fin[at(mine + lo, n2 - skip), (q // 2 % 2) * half:(q // 2 % 2 + 1) * half] = g1[q, skip:, :]

    def c6(base, side, dev):
        blk = fin.at[at(base + side * n_quarter, n_quarter)]
        return rdma(blk, blk, G0, side, side, dev)

    c6(mine, 0, up).start()
    c6(mine, 1, down).start()
    c6(other, 0, up).wait_recv()
    c6(other, 1, down).wait_recv()
    stores[2].start()

    @pl.when(x >= 2)
    def _():
        @pl.when(x == 2)
        def _():
            for piece in (0, 1):
                ag(x, x + 1, piece).wait_send()

    @pl.when(x < 2)
    def _():
        for piece in (0, 1):
            ag(x, x + 2, piece).wait_send()

    @pl.when(k == 0)
    def _():
        own_fwd.wait_send()

    @pl.when(k == 1)
    def _():
        to_sib(x).wait_send()

    def drain(v, carry):
        pass_on(v, k).wait_send()
        lift(v, mine).wait_send()
        lower(v, mine).wait_send()
        to_sib(v).wait_send()
        to_up(v).wait_send()
        to_down(v).wait_send()
        to_x(v, x).wait_send()
        return carry

    lax.fori_loop(0, x, drain, 0)
    to_up(x).wait_send()
    to_down(x).wait_send()
    for d in hops:
        c1((own + d) % 8, own).wait_send()
        c5((own + d) % 8, own).wait_send()
    for d in (1, 2, 3):
        c3((zo + d) % 4, zo).wait_send()
    c6(mine, 0, up).wait_send()
    c6(mine, 1, down).wait_send()
    for store in stores:
        store.wait()


def write_out(a, b, c, a_out, b_out, c_out, a_v, b_v, c_v, wide, sems):
    loads = [
        pltpu.make_async_copy(src, dst, sems.at[i])
        for i, (src, dst) in enumerate(((c, c_v), (b, b_v), (a, a_v)))
    ]
    stores = [
        pltpu.make_async_copy(src, dst, sems.at[3 + i])
        for i, (src, dst) in enumerate(((wide, c_out), (b_v, b_out), (a_v, a_out)))
    ]
    for load in loads:
        load.start()
    loads[0].wait()
    wide[...] = c_v[...].astype(F32)
    stores[0].start()
    for i in (1, 2):
        loads[i].wait()
        stores[i].start()
    for store in stores:
        store.wait()


def body(queries, latents, out_grad):
    rows, _, feat = queries.shape
    lat = out_grad.shape[2]
    n1 = feat // 4
    n2 = (n1 // 2 + 15) // 16 * 16
    half = rows // 2
    qt = queries.reshape(rows, feat).T
    vm = pltpu.VMEM
    shapes = (
        jax.ShapeDtypeStruct((rows, lat), BF),
        jax.ShapeDtypeStruct((feat, rows), F32),
    )
    results = pl.pallas_call(
        kernel,
        out_shape=shapes + (jax.ShapeDtypeStruct((feat, rows), BF),),
        in_specs=[pl.BlockSpec(memory_space=pl.ANY)] * 3,
        out_specs=[pl.BlockSpec(memory_space=pl.ANY)] * 3,
        scratch_shapes=[
            vm((rows, lat), BF),
            vm((feat, rows), F32),
            vm((feat, rows), BF),
            vm((feat, rows), BF),
            vm((feat, rows), BF),
            vm((rows, lat), BF),
            vm((8, feat, rows), BF),
            vm((rows, feat), BF),
            vm((lat, rows), BF),
            vm((8, rows, rows), F32),
            vm((8, rows, rows), F32),
            vm((rows, lat), F32),
            vm((rows, 1), F32),
            vm((rows, 1), F32),
            vm((4, feat, rows), BF),
            vm((4, feat, rows), BF),
            vm((4, feat, rows), F32),
            vm((4, feat // 2, rows), BF),
            vm((4, feat // 2, rows), BF),
            vm((4, feat // 2, rows), BF),
            vm((4, feat // 2, rows), BF),
            vm((feat // 2, rows), F32),
            vm((8, n2, half), BF),
            vm((8, n2, half), BF),
            vm((n2, half), F32),
            vm((4, n2, half), BF),
            vm((8, n2, half), BF),
            pltpu.SemaphoreType.DMA((3,)),
            pltpu.SemaphoreType.DMA((3,)),
            pltpu.SemaphoreType.DMA((26, 8)),
            pltpu.SemaphoreType.REGULAR,
        ],
        compiler_params=pltpu.CompilerParams(
            collective_id=0, has_side_effects=True, vmem_limit_bytes=60 * 2**20
        ),
    )(qt, latents.T, out_grad.reshape(rows, lat))
    att, qg, lg = pl.pallas_call(
        write_out,
        out_shape=shapes + (jax.ShapeDtypeStruct((feat, rows), F32),),
        in_specs=[pl.BlockSpec(memory_space=pl.ANY)] * 3,
        out_specs=[pl.BlockSpec(memory_space=pl.ANY)] * 3,
        scratch_shapes=[
            vm((rows, lat), BF),
            vm((feat, rows), F32),
            vm((feat, rows), BF),
            vm((feat, rows), F32),
            pltpu.SemaphoreType.DMA((6,)),
        ],
        compiler_params=pltpu.CompilerParams(vmem_limit_bytes=60 * 2**20),
    )(*results)
    return att.reshape(rows, 1, lat), qg.T.reshape(rows, 1, feat), lg.T


def solution(mesh):
    return jax.shard_map(
        body,
        mesh=mesh,
        in_specs=(
            P(("rep", "exp"), "ctx", None),
            P(("rep", "exp"), None),
            P(("rep", "exp"), "ctx", None),
        ),
        out_specs=(
            P(("rep", "exp"), "ctx", None),
            P(("rep", "exp"), "ctx", None),
            P(("rep", "exp"), None),
        ),
        check_vma=False,
    )
```

```python
import functools

import jax
import jax.numpy as jnp
from jax import lax
from jax.experimental import pallas as pl
from jax.experimental.pallas import tpu as pltpu
from jax.sharding import PartitionSpec as P

MESH = pl.DeviceIdType.MESH
BF = jnp.bfloat16
F32 = jnp.float32
score_scale = 192.0 ** (-0.5)
NN = (((1,), (0,)), ((), ()))
NT = (((1,), (1,)), ((), ()))
(AG, AH, ZU, ZD, FS, CR, RU, RD, XR, S1, S3, G1, G0) = range(0, 26, 2)


def mm(a, b, dims=NN):
    return lax.dot_general(a, b, dims, preferred_element_type=F32)


def at(start, size):
    return pl.ds(pl.multiple_of(start, 16), size)


def kernel(
    qt_any, lt_any, g_any,
    att_any, qg_any, lg_any,
    att_ref, qg_ref, fin,
    qt_ref, lt_ref, g_ref,
    keys, qn, gt, sc, pg, ctx, row_m, row_l,
    sib_out, sib_in, hold, z_out, z_in, x_out, x_in, total,
    s1_out, s1_in, part, s3, g1,
    in_sem, out_sem, sem, told,
):
    c = lax.axis_index("ctx")
    e = lax.axis_index("exp")
    yh, z = c // 16, c % 16
    zi, zo = z % 4, z // 4
    h, r = z % 2, zi // 2
    x, k = e // 2, e % 2
    feat, rows = lt_ref.shape
    lat = g_ref.shape[1]
    n_half, n_quarter = feat // 2, feat // 4
    mine, other = h * n_half, (1 - h) * n_half

    loads = [
        pltpu.make_async_copy(src, dst, in_sem.at[i])
        for i, (src, dst) in enumerate(((lt_any, lt_ref), (qt_any, qt_ref), (g_any, g_ref)))
    ]
    for load in loads:
        load.start()
    stores = [
        pltpu.make_async_copy(src, dst, out_sem.at[i])
        for i, (src, dst) in enumerate(((att_ref, att_any), (qg_ref, qg_any), (fin, lg_any)))
    ]

    sib = {"exp": x * 2 + (1 - k)}
    up, down = {"ctx": yh * 16 + (z + 1) % 16}, {"ctx": yh * 16 + (z + 15) % 16}
    def at_x(v):
        return {"exp": v * 2 + k}

    def at_shard(v):
        return {"ctx": (v // 2) * 16 + zo * 4 + (v % 2) * 2 + h}

    own = yh * 2 + r

    def at_zo(v):
        return {"ctx": yh * 16 + v * 4 + zi}

    def rdma(src, dst, kind, i, j, dev):
        return pltpu.make_async_remote_copy(
            src_ref=src, dst_ref=dst, send_sem=sem.at[kind, i], recv_sem=sem.at[kind + 1, j],
            device_id=dev, device_id_type=MESH,
        )

    barrier = pltpu.get_barrier_semaphore()
    def at_z(v):
        return {"ctx": yh * 16 + v % 16}

    def at_y(v):
        return {"ctx": (v % 4) * 16 + z}

    def tell(sem_ref, devices):
        for dev in devices:
            pl.semaphore_signal(sem_ref, inc=1, device_id=dev, device_id_type=MESH)

    near = [at_x((x + d) % 4) for d in (1, 2, 3)] + [sib, up, down, at_y(yh + 1), at_y(yh + 3)]
    tell(barrier, near)
    loads[0].wait()
    keys[e] = lt_ref[...]
    pl.semaphore_wait(barrier, len(near))
    tell(told.at[0], [up, down, at_y(yh + 1)])

    def ag(src_x, dst_x, piece):
        part = at(mine + piece * n_quarter, n_quarter)
        return rdma(
            lt_ref.at[part], keys.at[src_x * 2 + k, part], AG if piece == 0 else AH, dst_x, src_x, at_x(dst_x)
        )

    def pass_on(v, side):
        blk = keys.at[v * 2 + side]
        return rdma(blk, blk, FS, v, v, sib)

    def lift(v, base):
        blk = keys.at[v * 2 + k, at(base, n_quarter)]
        return rdma(blk, blk, ZU, v, v, up)

    def lower(v, base):
        blk = keys.at[v * 2 + k, at(base + n_quarter, n_quarter)]
        return rdma(blk, blk, ZD, v, v, down)

    own_fwd = rdma(lt_ref, keys.at[x * 2], FS, x, x, sib)

    for piece in (0, 1):
        @pl.when(x < 3)
        def _():
            ag(x, x + 1, piece).start()

        @pl.when(x == 0)
        def _():
            ag(x, x + 3, piece).start()

    @pl.when(k == 0)
    def _():
        own_fwd.start()

    loads[1].wait()
    qn[...] = qt_ref[...].T
    loads[2].wait()
    gt[...] = g_ref[...].T

    below = lax.broadcasted_iota(jnp.int32, (rows, rows), 1) <= lax.broadcasted_iota(jnp.int32, (rows, rows), 0)
    s = jnp.where(below, mm(qn[...], lt_ref[...]) * score_scale, -1e30)
    sc[e] = s
    m = jnp.max(s, axis=1, keepdims=True)
    p = jnp.exp(s - m)
    row_m[...] = m
    row_l[...] = jnp.sum(p, axis=1, keepdims=True)
    ctx[...] = mm(p.astype(BF), lt_ref[:lat, :], NT)
    pg[e] = mm(g_ref[...], lt_ref[:lat, :])

    @pl.when(x < 2)
    def _():
        for piece in (0, 1):
            ag(x, x + 1, piece).wait_send()

            @pl.when(x == 0)
            def _():
                ag(x, x + 3, piece).wait_send()

            ag(x, x + 2, piece).start()

    def forward(j):
        s = mm(qn[...], keys[j]) * score_scale
        sc[j] = s
        m_old = row_m[...]
        m = jnp.maximum(m_old, jnp.max(s, axis=1, keepdims=True))
        p = jnp.exp(s - m)
        fade = jnp.exp(m_old - m)
        row_m[...] = m
        row_l[...] = row_l[...] * fade + jnp.sum(p, axis=1, keepdims=True)
        ctx[...] = ctx[...] * fade + mm(p.astype(BF), keys[j, :lat, :], NT)
        pg[j] = mm(g_ref[...], keys[j, :lat, :])

    @pl.when(k == 1)
    def _():
        own_fwd.wait_recv()
        forward(x * 2)

    def source(i):
        return x - jnp.where(i == 0, 1, jnp.where(i == 1, 3, 2))

    def share_step(i, carry):
        v = source(i)

        @pl.when(v >= 0)
        def _():
            ag(v, x, 0).wait_recv()
            lift(v, mine).start()
            ag(v, x, 1).wait_recv()
            lower(v, mine).start()

        return carry

    lax.fori_loop(0, 3, share_step, 0)

    def gather_step(i, carry):
        v = source(i)

        @pl.when((i < 3) & (v >= 0))
        def _():
            lift(v, other).wait_recv()
            lower(v, other).wait_recv()
            pass_on(v, k).start()

        w = source(i - 1)

        @pl.when((i > 0) & (w >= 0))
        def _():
            forward(w * 2 + k)
            pass_on(w, 1 - k).wait_recv()
            forward(w * 2 + 1 - k)

        return carry

    lax.fori_loop(0, 4, gather_step, 0)
    pl.semaphore_wait(told.at[0], 3)
    tell(told.at[1], [at_y(yh + 1), at_y(yh + 2), at_y(yh + 3), at_z(z + 2), at_z(z + 14)])

    inv = 1.0 / row_l[...]
    context = ctx[...] * inv
    att_ref[...] = context.astype(BF)
    stores[0].start()
    lse = row_m[...] + jnp.log(row_l[...])
    delta = jnp.sum(g_ref[...].astype(F32) * context, axis=1, keepdims=True)
    row_m[...] = lse
    row_l[...] = delta
    qg_ref[...] = jnp.zeros_like(qg_ref)

    def backward(j, store):
        p = jnp.exp(sc[j] - row_m[...])
        ds = (p * (pg[j] - row_l[...])).astype(BF)
        qg_ref[...] += mm(keys[j], ds, NT)
        store(0, lat, mm(qt_ref[:lat, :], ds) * score_scale + mm(gt[...], p.astype(BF)))
        store(lat, feat, mm(qt_ref[lat:, :], ds) * score_scale)

    def to_sib(v):
        return rdma(sib_out.at[v], sib_in.at[v], CR, v, v, sib)

    def to_up(v):
        return rdma(z_out.at[v, pl.ds(n_quarter, n_quarter)], z_in.at[v, pl.ds(n_quarter, n_quarter)], RU, v, v, up)

    def to_down(v):
        return rdma(z_out.at[v, pl.ds(0, n_quarter)], z_in.at[v, pl.ds(0, n_quarter)], RD, v, v, down)

    def to_x(v, src):
        return rdma(x_out.at[v], x_in.at[src], XR, v, src, at_x(v))

    def order(i):
        return x - jnp.where(i == 0, 2, jnp.where(i == 1, 3, jnp.where(i == 2, 1, 0)))

    def share_sum(u):
        @pl.when(u * 2 + k <= x * 2 + 1 - k)
        def _():
            to_sib(u).wait_recv()
            hold[u] += sib_in[u].astype(F32)

        z_out[u] = hold[u, at(other, n_half), :].astype(BF)
        to_up(u).start()
        to_down(u).start()

    def bwd_step(i, carry):
        v = order(i)

        @pl.when(v >= 0)
        def _():
            def put_sib(lo, hi, val):
                sib_out[v, lo:hi, :] = val.astype(BF)

            def put_hold(lo, hi, val):
                hold[v, lo:hi, :] = val

            @pl.when(v * 2 + 1 - k <= e)
            def _():
                backward(v * 2 + 1 - k, put_sib)
                to_sib(v).start()

            backward(v * 2 + k, put_hold)

        u = order(i - 1)

        @pl.when((i > 0) & (u >= 0))
        def _():
            share_sum(u)

        return carry

    lax.fori_loop(0, 4, bwd_step, 0)

    def send_step(i, carry):
        t = order(i)

        @pl.when(i == 2)
        def _():
            share_sum(x)

        @pl.when(t >= 0)
        def _():
            to_down(t).wait_recv()
            to_up(t).wait_recv()
            val = hold[t, at(mine, n_half), :] + z_in[t].astype(F32)

            @pl.when(t < x)
            def _():
                x_out[t] = val.astype(BF)
                to_x(t, x).start()

            @pl.when(t == x)
            def _():
                total[...] = val

        return carry

    lax.fori_loop(0, 4, send_step, 0)
    pl.semaphore_wait(told.at[1], 5)
    tell(told.at[2], [at_z(z + 4)])
    qg_ref[...] = qg_ref[...] * score_scale
    stores[1].start()

    def add_x(i, carry):
        v = 3 - i
        to_x(x, v).wait_recv()
        total[...] += x_in[v].astype(F32)
        return carry

    lax.fori_loop(0, 3 - x, add_x, 0)

    half = rows // 2
    n1, n2 = n_half // 2, s1_out.shape[1]

    def c1(peer, src):
        return rdma(s1_out.at[peer], s1_in.at[src], S1, peer, src, at_shard(peer))

    for q in range(8):
        lo = (q // 4) * n1 + (q % 2) * (n1 - n2)
        val = total[lo:lo + n2, (q // 2 % 2) * half:(q // 2 % 2 + 1) * half]
        s1_out[q] = val.astype(BF)

        @pl.when(own == q)
        def _():
            part[...] = val

    hops = (4, 5, 3, 2, 6, 7, 1)
    for d in hops:
        c1((own + d) % 8, own).start()
    for d in hops[::-1]:
        v = (own + d) % 8
        c1(own, v).wait_recv()
        part[...] += s1_in[v].astype(F32)

    def c3(peer, src):
        return rdma(s3.at[src], s3.at[src], S3, peer, src, at_zo(peer))

    s3[zo] = part[...].astype(BF)
    pl.semaphore_wait(told.at[2], 1)
    for d in (2, 1, 3):
        c3((zo + d) % 4, zo).start()
    for d in (1, 3, 2):
        c3(zo, (zo + d) % 4).wait_recv()
    g1[own] = (s3[0].astype(F32) + s3[1].astype(F32) + s3[2].astype(F32) + s3[3].astype(F32)).astype(BF)

    def c5(peer, src):
        return rdma(g1.at[src], g1.at[src], G1, peer, src, at_shard(peer))

    for d in hops:
        c5((own + d) % 8, own).start()
    for d in hops[::-1]:
        c5(own, (own + d) % 8).wait_recv()
    for q in range(8):
        skip = 0 if q % 2 == 0 else 2 * n2 - n1
        lo = (q // 4) * n1 + (q % 2) * n2
        fin[at(mine + lo, n2 - skip), (q // 2 % 2) * half:(q // 2 % 2 + 1) * half] = g1[q, skip:, :]

    def c6(base, side, dev):
        blk = fin.at[at(base + side * n_quarter, n_quarter)]
        return rdma(blk, blk, G0, side, side, dev)

    c6(mine, 0, up).start()
    c6(mine, 1, down).start()
    c6(other, 0, up).wait_recv()
    c6(other, 1, down).wait_recv()
    stores[2].start()

    @pl.when(x >= 2)
    def _():
        @pl.when(x == 2)
        def _():
            for piece in (0, 1):
                ag(x, x + 1, piece).wait_send()

    @pl.when(x < 2)
    def _():
        for piece in (0, 1):
            ag(x, x + 2, piece).wait_send()

    @pl.when(k == 0)
    def _():
        own_fwd.wait_send()

    @pl.when(k == 1)
    def _():
        to_sib(x).wait_send()

    def drain(v, carry):
        pass_on(v, k).wait_send()
        lift(v, mine).wait_send()
        lower(v, mine).wait_send()
        to_sib(v).wait_send()
        to_up(v).wait_send()
        to_down(v).wait_send()
        to_x(v, x).wait_send()
        return carry

    lax.fori_loop(0, x, drain, 0)
    to_up(x).wait_send()
    to_down(x).wait_send()
    for d in hops:
        c1((own + d) % 8, own).wait_send()
        c5((own + d) % 8, own).wait_send()
    for d in (1, 2, 3):
        c3((zo + d) % 4, zo).wait_send()
    c6(mine, 0, up).wait_send()
    c6(mine, 1, down).wait_send()
    for store in stores:
        store.wait()


def write_out(a, b, c, a_out, b_out, c_out, a_v, b_v, c_v, wide, sems):
    loads = [
        pltpu.make_async_copy(src, dst, sems.at[i])
        for i, (src, dst) in enumerate(((c, c_v), (b, b_v), (a, a_v)))
    ]
    stores = [
        pltpu.make_async_copy(src, dst, sems.at[3 + i])
        for i, (src, dst) in enumerate(((wide, c_out), (b_v, b_out), (a_v, a_out)))
    ]
    for load in loads:
        load.start()
    loads[0].wait()
    wide[...] = c_v[...].astype(F32)
    stores[0].start()
    for i in (1, 2):
        loads[i].wait()
        stores[i].start()
    for store in stores:
        store.wait()


def body(queries, latents, out_grad):
    rows, _, feat = queries.shape
    lat = out_grad.shape[2]
    n1 = feat // 4
    n2 = (n1 // 2 + 15) // 16 * 16
    half = rows // 2
    qt = queries.reshape(rows, feat).T
    vm = pltpu.VMEM
    shapes = (
        jax.ShapeDtypeStruct((rows, lat), BF),
        jax.ShapeDtypeStruct((feat, rows), F32),
    )
    results = pl.pallas_call(
        kernel,
        out_shape=shapes + (jax.ShapeDtypeStruct((feat, rows), BF),),
        in_specs=[pl.BlockSpec(memory_space=pl.ANY)] * 3,
        out_specs=[pl.BlockSpec(memory_space=pl.ANY)] * 3,
        scratch_shapes=[
            vm((rows, lat), BF),
            vm((feat, rows), F32),
            vm((feat, rows), BF),
            vm((feat, rows), BF),
            vm((feat, rows), BF),
            vm((rows, lat), BF),
            vm((8, feat, rows), BF),
            vm((rows, feat), BF),
            vm((lat, rows), BF),
            vm((8, rows, rows), F32),
            vm((8, rows, rows), F32),
            vm((rows, lat), F32),
            vm((rows, 1), F32),
            vm((rows, 1), F32),
            vm((4, feat, rows), BF),
            vm((4, feat, rows), BF),
            vm((4, feat, rows), F32),
            vm((4, feat // 2, rows), BF),
            vm((4, feat // 2, rows), BF),
            vm((4, feat // 2, rows), BF),
            vm((4, feat // 2, rows), BF),
            vm((feat // 2, rows), F32),
            vm((8, n2, half), BF),
            vm((8, n2, half), BF),
            vm((n2, half), F32),
            vm((4, n2, half), BF),
            vm((8, n2, half), BF),
            pltpu.SemaphoreType.DMA((3,)),
            pltpu.SemaphoreType.DMA((3,)),
            pltpu.SemaphoreType.DMA((26, 8)),
            pltpu.SemaphoreType.REGULAR((3,)),
        ],
        compiler_params=pltpu.CompilerParams(
            collective_id=0, has_side_effects=True, vmem_limit_bytes=60 * 2**20
        ),
    )(qt, latents.T, out_grad.reshape(rows, lat))
    att, qg, lg = pl.pallas_call(
        write_out,
        out_shape=shapes + (jax.ShapeDtypeStruct((feat, rows), F32),),
        in_specs=[pl.BlockSpec(memory_space=pl.ANY)] * 3,
        out_specs=[pl.BlockSpec(memory_space=pl.ANY)] * 3,
        scratch_shapes=[
            vm((rows, lat), BF),
            vm((feat, rows), F32),
            vm((feat, rows), BF),
            vm((feat, rows), F32),
            pltpu.SemaphoreType.DMA((6,)),
        ],
        compiler_params=pltpu.CompilerParams(vmem_limit_bytes=60 * 2**20),
    )(*results)
    return att.reshape(rows, 1, lat), qg.T.reshape(rows, 1, feat), lg.T


def solution(mesh):
    return jax.shard_map(
        body,
        mesh=mesh,
        in_specs=(
            P(("rep", "exp"), "ctx", None),
            P(("rep", "exp"), None),
            P(("rep", "exp"), "ctx", None),
        ),
        out_specs=(
            P(("rep", "exp"), "ctx", None),
            P(("rep", "exp"), "ctx", None),
            P(("rep", "exp"), None),
        ),
        check_vma=False,
    )
```

```python
import functools

import jax
import jax.numpy as jnp
from jax import lax
from jax.experimental import pallas as pl
from jax.experimental.pallas import tpu as pltpu
from jax.sharding import PartitionSpec as P

MESH = pl.DeviceIdType.MESH
BF = jnp.bfloat16
F32 = jnp.float32
score_scale = 192.0 ** (-0.5)
NN = (((1,), (0,)), ((), ()))
NT = (((1,), (1,)), ((), ()))
(AG, AH, ZU, ZD, FS, CR, RU, RD, XR, XQ, S1, S3, G1, G0) = range(0, 28, 2)


def mm(a, b, dims=NN):
    return lax.dot_general(a, b, dims, preferred_element_type=F32)


def at(start, size):
    return pl.ds(pl.multiple_of(start, 16), size)


def kernel(
    qt_any, lt_any, g_any,
    att_any, qg_any, lg_any,
    att_ref, qg_ref, fin,
    qt_ref, lt_ref, g_ref,
    keys, qn, gt, sc, pg, ctx, row_m, row_l,
    sib_out, sib_in, hold, z_out, z_in, x_out, x_in, total,
    s1_out, s1_in, part, s3, g1, g0,
    in_sem, out_sem, sem, told,
):
    c = lax.axis_index("ctx")
    e = lax.axis_index("exp")
    yh, z = c // 16, c % 16
    zi, zo = z % 4, z // 4
    h, r = z % 2, zi // 2
    x, k = e // 2, e % 2
    feat, rows = lt_ref.shape
    lat = g_ref.shape[1]
    n_half, n_quarter = feat // 2, feat // 4
    mine, other = h * n_half, (1 - h) * n_half

    loads = [
        pltpu.make_async_copy(src, dst, in_sem.at[i])
        for i, (src, dst) in enumerate(((lt_any, lt_ref), (qt_any, qt_ref), (g_any, g_ref)))
    ]
    for load in loads:
        load.start()
    stores = [
        pltpu.make_async_copy(src, dst, out_sem.at[i])
        for i, (src, dst) in enumerate(((att_ref, att_any), (qg_ref, qg_any), (fin, lg_any)))
    ]

    sib = {"exp": x * 2 + (1 - k)}
    up, down = {"ctx": yh * 16 + (z + 1) % 16}, {"ctx": yh * 16 + (z + 15) % 16}
    def at_x(v):
        return {"exp": v * 2 + k}

    def at_shard(v):
        return {"ctx": (v // 2) * 16 + zo * 4 + (v % 2) * 2 + h}

    own = yh * 2 + r

    def at_zo(v):
        return {"ctx": yh * 16 + v * 4 + zi}

    def rdma(src, dst, kind, i, j, dev):
        return pltpu.make_async_remote_copy(
            src_ref=src, dst_ref=dst, send_sem=sem.at[kind, i], recv_sem=sem.at[kind + 1, j],
            device_id=dev, device_id_type=MESH,
        )

    barrier = pltpu.get_barrier_semaphore()
    def at_z(v):
        return {"ctx": yh * 16 + v % 16}

    def at_y(v):
        return {"ctx": (v % 4) * 16 + z}

    def tell(sem_ref, devices):
        for dev in devices:
            pl.semaphore_signal(sem_ref, inc=1, device_id=dev, device_id_type=MESH)

    near = [at_x((x + d) % 4) for d in (1, 2, 3)] + [sib, up, down, at_y(yh + 1), at_y(yh + 3)]
    tell(barrier, near)
    loads[0].wait()
    keys[e] = lt_ref[...]
    pl.semaphore_wait(barrier, len(near))
    tell(told.at[0], [up, down, at_y(yh + 1)])

    def ag(src_x, dst_x, piece):
        part = at(mine + piece * n_quarter, n_quarter)
        return rdma(
            lt_ref.at[part], keys.at[src_x * 2 + k, part], AG if piece == 0 else AH, dst_x, src_x, at_x(dst_x)
        )

    def pass_on(v, side):
        blk = keys.at[v * 2 + side]
        return rdma(blk, blk, FS, v, v, sib)

    def lift(v, base):
        blk = keys.at[v * 2 + k, at(base, n_quarter)]
        return rdma(blk, blk, ZU, v, v, up)

    def lower(v, base):
        blk = keys.at[v * 2 + k, at(base + n_quarter, n_quarter)]
        return rdma(blk, blk, ZD, v, v, down)

    own_fwd = rdma(lt_ref, keys.at[x * 2], FS, x, x, sib)

    for piece in (0, 1):
        @pl.when(x < 3)
        def _():
            ag(x, x + 1, piece).start()

        @pl.when(x == 0)
        def _():
            ag(x, x + 3, piece).start()

    @pl.when(k == 0)
    def _():
        own_fwd.start()

    loads[1].wait()
    qn[...] = qt_ref[...].T
    loads[2].wait()
    gt[...] = g_ref[...].T

    below = lax.broadcasted_iota(jnp.int32, (rows, rows), 1) <= lax.broadcasted_iota(jnp.int32, (rows, rows), 0)
    s = jnp.where(below, mm(qn[...], lt_ref[...]) * score_scale, -1e30)
    sc[e] = s
    m = jnp.max(s, axis=1, keepdims=True)
    p = jnp.exp(s - m)
    row_m[...] = m
    row_l[...] = jnp.sum(p, axis=1, keepdims=True)
    ctx[...] = mm(p.astype(BF), lt_ref[:lat, :], NT)
    pg[e] = mm(g_ref[...], lt_ref[:lat, :])

    @pl.when(x < 2)
    def _():
        for piece in (0, 1):
            ag(x, x + 1, piece).wait_send()

            @pl.when(x == 0)
            def _():
                ag(x, x + 3, piece).wait_send()

            ag(x, x + 2, piece).start()

    def forward(j):
        s = mm(qn[...], keys[j]) * score_scale
        sc[j] = s
        m_old = row_m[...]
        m = jnp.maximum(m_old, jnp.max(s, axis=1, keepdims=True))
        p = jnp.exp(s - m)
        fade = jnp.exp(m_old - m)
        row_m[...] = m
        row_l[...] = row_l[...] * fade + jnp.sum(p, axis=1, keepdims=True)
        ctx[...] = ctx[...] * fade + mm(p.astype(BF), keys[j, :lat, :], NT)
        pg[j] = mm(g_ref[...], keys[j, :lat, :])

    @pl.when(k == 1)
    def _():
        own_fwd.wait_recv()
        forward(x * 2)

    def source(i):
        return x - jnp.where(i == 0, 1, jnp.where(i == 1, 3, 2))

    def share_step(i, carry):
        v = source(i)

        @pl.when(v >= 0)
        def _():
            ag(v, x, 0).wait_recv()
            lift(v, mine).start()
            ag(v, x, 1).wait_recv()
            lower(v, mine).start()

        return carry

    lax.fori_loop(0, 3, share_step, 0)

    def gather_step(i, carry):
        v = source(i)

        @pl.when((i < 3) & (v >= 0))
        def _():
            lift(v, other).wait_recv()
            lower(v, other).wait_recv()
            pass_on(v, k).start()

        w = source(i - 1)

        @pl.when((i > 0) & (w >= 0))
        def _():
            forward(w * 2 + k)
            pass_on(w, 1 - k).wait_recv()
            forward(w * 2 + 1 - k)

        return carry

    lax.fori_loop(0, 4, gather_step, 0)
    pl.semaphore_wait(told.at[0], 3)
    tell(told.at[1], [at_y(yh + 1), at_y(yh + 2), at_y(yh + 3), at_z(z + 2), at_z(z + 14)])

    inv = 1.0 / row_l[...]
    context = ctx[...] * inv
    att_ref[...] = context.astype(BF)
    stores[0].start()
    lse = row_m[...] + jnp.log(row_l[...])
    delta = jnp.sum(g_ref[...].astype(F32) * context, axis=1, keepdims=True)
    row_m[...] = lse
    row_l[...] = delta
    qg_ref[...] = jnp.zeros_like(qg_ref)

    def backward(j, store):
        p = jnp.exp(sc[j] - row_m[...])
        ds = (p * (pg[j] - row_l[...])).astype(BF)
        qg_ref[...] += mm(keys[j], ds, NT)
        store(0, lat, mm(qt_ref[:lat, :], ds) * score_scale + mm(gt[...], p.astype(BF)))
        store(lat, feat, mm(qt_ref[lat:, :], ds) * score_scale)

    def to_sib(v):
        return rdma(sib_out.at[v], sib_in.at[v], CR, v, v, sib)

    def to_up(v):
        return rdma(z_out.at[v, pl.ds(n_quarter, n_quarter)], z_in.at[v, pl.ds(n_quarter, n_quarter)], RU, v, v, up)

    def to_down(v):
        return rdma(z_out.at[v, pl.ds(0, n_quarter)], z_in.at[v, pl.ds(0, n_quarter)], RD, v, v, down)

    def to_x(v, src, piece):
        part = pl.ds(piece * n_quarter, n_quarter)
        return rdma(x_out.at[v, part], x_in.at[src, part], XR if piece == 0 else XQ, v, src, at_x(v))

    def order(i):
        return x - jnp.where(i == 0, 2, jnp.where(i == 1, 3, jnp.where(i == 2, 1, 0)))

    def share_sum(u):
        @pl.when(u * 2 + k <= x * 2 + 1 - k)
        def _():
            to_sib(u).wait_recv()
            hold[u] += sib_in[u].astype(F32)

        z_out[u] = hold[u, at(other, n_half), :].astype(BF)
        to_up(u).start()
        to_down(u).start()

    def sib_step(i, carry):
        v = order(i)

        @pl.when((v >= 0) & (v * 2 + 1 - k <= e))
        def _():
            def put_sib(lo, hi, val):
                sib_out[v, lo:hi, :] = val.astype(BF)

            backward(v * 2 + 1 - k, put_sib)
            to_sib(v).start()

        return carry

    lax.fori_loop(0, 4, sib_step, 0)

    def own_step(i, carry):
        v = order(i)

        @pl.when(v >= 0)
        def _():
            def put_hold(lo, hi, val):
                hold[v, lo:hi, :] = val

            backward(v * 2 + k, put_hold)

            @pl.when(v < x)
            def _():
                share_sum(v)

        return carry

    lax.fori_loop(0, 4, own_step, 0)

    def pair_sum(t, piece):
        lo = piece * n_quarter
        return hold[t, at(mine + lo, n_quarter), :] + z_in[t, lo:lo + n_quarter, :].astype(F32)

    def send_step(piece):
        def step(i, carry):
            t = order(i)

            @pl.when(t >= 0)
            def _():
                (to_down, to_up)[piece](t).wait_recv()
                x_out[t, piece * n_quarter:(piece + 1) * n_quarter, :] = pair_sum(t, piece).astype(BF)
                to_x(t, x, piece).start()

            return carry

        lax.fori_loop(0, 3, step, 0)

    send_step(0)
    share_sum(x)
    send_step(1)
    pl.semaphore_wait(told.at[1], 5)
    tell(told.at[2], [at_z(z + 4)])
    qg_ref[...] = qg_ref[...] * score_scale
    stores[1].start()

    to_down(x).wait_recv()
    total[:n_quarter, :] = pair_sum(x, 0)
    to_up(x).wait_recv()
    total[n_quarter:, :] = pair_sum(x, 1)

    half = rows // 2
    n1, n2 = n_quarter, s1_out.shape[1]

    def c1(peer, src):
        return rdma(s1_out.at[peer], s1_in.at[src], S1, peer, src, at_shard(peer))

    for piece in (0, 1):
        span = slice(piece * n_quarter, (piece + 1) * n_quarter)

        def add_x(i, carry):
            v = 3 - i
            to_x(x, v, piece).wait_recv()
            total[span, :] += x_in[v, span, :].astype(F32)
            return carry

        lax.fori_loop(0, 3 - x, add_x, 0)
        for q in range(piece * 4, piece * 4 + 4):
            lo = piece * n1 + (q % 2) * (n1 - n2)
            val = total[lo:lo + n2, (q // 2 % 2) * half:(q // 2 % 2 + 1) * half]

            @pl.when(own == q)
            def _():
                part[...] = val

            @pl.when(own != q)
            def _():
                s1_out[q] = val.astype(BF)
                c1(q, own).start()

    hops = (4, 5, 3, 2, 6, 7, 1)
    for d in hops[::-1]:
        v = (own + d) % 8
        c1(own, v).wait_recv()
        part[...] += s1_in[v].astype(F32)

    def c3(peer, src):
        return rdma(s3.at[src], s3.at[src], S3, peer, src, at_zo(peer))

    s3[zo] = part[...].astype(BF)
    pl.semaphore_wait(told.at[2], 1)
    @pl.when(zo != 0)
    def _():
        c3(0, zo).start()
        c3(0, zo).wait_send()

    for q in (1, 2, 3):
        @pl.when(zo != q)
        def _():
            c3(q, zo).start()
    @pl.when(x >= 2)
    def _():
        @pl.when(x == 2)
        def _():
            for piece in (0, 1):
                ag(x, x + 1, piece).wait_send()

    @pl.when(x < 2)
    def _():
        for piece in (0, 1):
            ag(x, x + 2, piece).wait_send()

    @pl.when(k == 0)
    def _():
        own_fwd.wait_send()

    @pl.when(k == 1)
    def _():
        to_sib(x).wait_send()

    def drain(v, carry):
        pass_on(v, k).wait_send()
        lift(v, mine).wait_send()
        lower(v, mine).wait_send()
        to_sib(v).wait_send()
        to_up(v).wait_send()
        to_down(v).wait_send()
        to_x(v, x, 0).wait_send()
        to_x(v, x, 1).wait_send()
        return carry

    lax.fori_loop(0, x, drain, 0)
    to_up(x).wait_send()
    to_down(x).wait_send()
    for d in hops:
        c1((own + d) % 8, own).wait_send()
    stores[0].wait()
    stores[1].wait()
    for d in (1, 3, 2):
        c3(zo, (zo + d) % 4).wait_recv()
    g1[own] = (s3[0].astype(F32) + s3[1].astype(F32) + s3[2].astype(F32) + s3[3].astype(F32)).astype(BF)

    def c5(peer, src):
        return rdma(g1.at[src], g1.at[src], G1, peer, src, at_shard(peer))

    def c6(q, dev):
        return rdma(g1.at[q], g0.at[q], G0, q, q, dev)

    def relay(q):
        @pl.when(q < 4)
        def _():
            c6(q, up).start()

        @pl.when(q >= 4)
        def _():
            c6(q, down).start()

    for d in hops:
        c5((own + d) % 8, own).start()
    relay(own)
    for d in hops[::-1]:
        v = (own + d) % 8
        c5(own, v).wait_recv()
        relay(v)

    def place(base, shards, q):
        skip = 0 if q % 2 == 0 else 2 * n2 - n1
        lo = (q // 4) * n1 + (q % 2) * n2
        fin[at(base + lo, n2 - skip), (q // 2 % 2) * half:(q // 2 % 2 + 1) * half] = shards[q, skip:, :]

    for q in range(8):
        place(mine, g1, q)
    for q in range(8):
        c6(q, up if q < 4 else down).wait_recv()
        place(other, g0, q)
    stores[2].start()

    for d in hops:
        c5((own + d) % 8, own).wait_send()
    for q in (1, 2, 3):
        @pl.when(zo != q)
        def _():
            c3(q, zo).wait_send()

    for q in range(8):
        c6(q, up if q < 4 else down).wait_send()
    stores[2].wait()


def write_out(a, b, c, a_out, b_out, c_out, a_v, b_v, c_v, wide, sems):
    loads = [
        pltpu.make_async_copy(src, dst, sems.at[i])
        for i, (src, dst) in enumerate(((c, c_v), (b, b_v), (a, a_v)))
    ]
    stores = [
        pltpu.make_async_copy(src, dst, sems.at[3 + i])
        for i, (src, dst) in enumerate(((wide, c_out), (b_v, b_out), (a_v, a_out)))
    ]
    for load in loads:
        load.start()
    loads[0].wait()
    wide[...] = c_v[...].astype(F32)
    stores[0].start()
    for i in (1, 2):
        loads[i].wait()
        stores[i].start()
    for store in stores:
        store.wait()


def body(queries, latents, out_grad):
    rows, _, feat = queries.shape
    lat = out_grad.shape[2]
    n1 = feat // 4
    n2 = (n1 // 2 + 15) // 16 * 16
    half = rows // 2
    qt = queries.reshape(rows, feat).T
    vm = pltpu.VMEM
    shapes = (
        jax.ShapeDtypeStruct((rows, lat), BF),
        jax.ShapeDtypeStruct((feat, rows), F32),
    )
    results = pl.pallas_call(
        kernel,
        out_shape=shapes + (jax.ShapeDtypeStruct((feat, rows), BF),),
        in_specs=[pl.BlockSpec(memory_space=pl.ANY)] * 3,
        out_specs=[pl.BlockSpec(memory_space=pl.ANY)] * 3,
        scratch_shapes=[
            vm((rows, lat), BF),
            vm((feat, rows), F32),
            vm((feat, rows), BF),
            vm((feat, rows), BF),
            vm((feat, rows), BF),
            vm((rows, lat), BF),
            vm((8, feat, rows), BF),
            vm((rows, feat), BF),
            vm((lat, rows), BF),
            vm((8, rows, rows), F32),
            vm((8, rows, rows), F32),
            vm((rows, lat), F32),
            vm((rows, 1), F32),
            vm((rows, 1), F32),
            vm((4, feat, rows), BF),
            vm((4, feat, rows), BF),
            vm((4, feat, rows), F32),
            vm((4, feat // 2, rows), BF),
            vm((4, feat // 2, rows), BF),
            vm((4, feat // 2, rows), BF),
            vm((4, feat // 2, rows), BF),
            vm((feat // 2, rows), F32),
            vm((8, n2, half), BF),
            vm((8, n2, half), BF),
            vm((n2, half), F32),
            vm((4, n2, half), BF),
            vm((8, n2, half), BF),
            vm((8, n2, half), BF),
            pltpu.SemaphoreType.DMA((3,)),
            pltpu.SemaphoreType.DMA((3,)),
            pltpu.SemaphoreType.DMA((28, 8)),
            pltpu.SemaphoreType.REGULAR((3,)),
        ],
        compiler_params=pltpu.CompilerParams(
            collective_id=0, has_side_effects=True, vmem_limit_bytes=60 * 2**20
        ),
    )(qt, latents.T, out_grad.reshape(rows, lat))
    att, qg, lg = pl.pallas_call(
        write_out,
        out_shape=shapes + (jax.ShapeDtypeStruct((feat, rows), F32),),
        in_specs=[pl.BlockSpec(memory_space=pl.ANY)] * 3,
        out_specs=[pl.BlockSpec(memory_space=pl.ANY)] * 3,
        scratch_shapes=[
            vm((rows, lat), BF),
            vm((feat, rows), F32),
            vm((feat, rows), BF),
            vm((feat, rows), F32),
            pltpu.SemaphoreType.DMA((6,)),
        ],
        compiler_params=pltpu.CompilerParams(vmem_limit_bytes=60 * 2**20),
    )(*results)
    return att.reshape(rows, 1, lat), qg.T.reshape(rows, 1, feat), lg.T


def solution(mesh):
    return jax.shard_map(
        body,
        mesh=mesh,
        in_specs=(
            P(("rep", "exp"), "ctx", None),
            P(("rep", "exp"), None),
            P(("rep", "exp"), "ctx", None),
        ),
        out_specs=(
            P(("rep", "exp"), "ctx", None),
            P(("rep", "exp"), "ctx", None),
            P(("rep", "exp"), None),
        ),
        check_vma=False,
    )
```
